32 devices in a mesh: groups: 2 (over x), blk: 16 (over z, y, core).
Axes of the slice: x: 2, y: 2, z: 4, core: 2. Of those that a mesh axis runs over, the one named last changes fastest.
Arguments:
- ocean_fields: float32 [8, 2048, 8, 128], P(None, ('groups', 'blk')), parts along dimension 1, may hold values from -1.5 to 8, as said below
- stress_in: float32 [3, 256, 4096], P(None, ('groups', 'blk')), parts along dimension 1, may hold values from -3 to 3
- ocean_slot: int32 [512], replicated, may hold values from 0 to 1023, as said below
- ice_mask: int32 [512], replicated, may hold values 0 or 1
Outputs:
- velocity_out: float32 [2, 2048, 8, 128], P(None, ('groups', 'blk')), parts along dimension 1
- stress_out: float32 [3, 256, 4096], P(None, ('groups', 'blk')), parts along dimension 1
The draws below stay inside these ranges and needn't reach their ends.
There are 2 independent parts, one for each index of `groups`. The reference program is written for one: setup_inputs(seed, part) draws one part's arguments, and reference() takes and returns one part's arrays. A program takes and returns all parts, laid end to end along the dimension named above; an argument that names none is the same for every part. Nothing has to cross between parts.
Inputs may be any that keep to these rules, and one draw needn't show every extreme that they name: Entries are distinct. Ice block i lies in slot ocean_slot[i] % 64 of ocean owner ocean_slot[i] // 64. Among the 32 ice blocks sharing i // 32, each ocean owner holds none or exactly 4; ocean owner 16 - 1 holds 64 ice blocks in all, one in each of its slots. `ocean_fields`: fields 0, 1, 4, 5, 6, 7 lie within -1.5 to 1.5; field 2 within 0.1 to 8; field 3 within 0.5 to 4.
All inputs are finite; a program needn't handle non-finite values.
Results may differ from the reference program's by a relative error of at most 0.000033.
Values sent between devices are 32-bit elements; how exact they have to be, the bound alone decides.
A program may use at most 64 MiB of HBM per device.

```python
import math
import jax
import jax.numpy as jnp
from jax import lax

BY = 8
BX = 128
KB = 32
ITERS = 6
OWNERS = 16
OB_DEV = 64
PAIR_CAP = 4
NI = 512
NOS = 1024
NIR = 128
NIC = 4096


def draw_ocean_fields(key, part):
    key = jax.random.fold_in(key, 5)
    subkeys = jax.random.split(key, 8)
    cell_shape = (NOS, BY, BX)
    vel_x = jnp.clip(0.3 * jax.random.normal(subkeys[0], cell_shape), -1.5, 1.5)
    vel_y = jnp.clip(0.3 * jax.random.normal(subkeys[1], cell_shape), -1.5, 1.5)
    strength = jnp.exp(jax.random.uniform(subkeys[2], cell_shape, minval=math.log(0.2), maxval=math.log(5.0)))
    ice_mass = jnp.exp(jax.random.uniform(subkeys[3], cell_shape, minval=math.log(0.5), maxval=math.log(4.0)))
    wind_x = jnp.clip(0.4 * jax.random.normal(subkeys[4], cell_shape), -1.5, 1.5)
    wind_y = jnp.clip(0.4 * jax.random.normal(subkeys[5], cell_shape), -1.5, 1.5)
    current_x = jnp.clip(0.3 * jax.random.normal(subkeys[6], cell_shape), -1.5, 1.5)
    current_y = jnp.clip(0.3 * jax.random.normal(subkeys[7], cell_shape), -1.5, 1.5)
    return jnp.stack([vel_x, vel_y, strength, ice_mass, wind_x, wind_y, current_x, current_y]).astype(jnp.float32)


def draw_ocean_slot(key, part):
    key = jax.random.fold_in(key, 11)
    subkeys = jax.random.split(key, 4)
    owner_rank = jax.random.permutation(subkeys[0], OWNERS).astype(jnp.int32)
    owner_bias = jnp.where(jnp.arange(OWNERS, dtype=jnp.int32) == OWNERS - 1, 4 * OWNERS, owner_rank)
    noise_draw = jax.random.randint(subkeys[1], (OWNERS, OWNERS), 0, OWNERS)
    owner_score = (noise_draw + owner_bias[None, :]) * OWNERS + jnp.arange(OWNERS, dtype=jnp.int32)[None, :]
    chosen = lax.top_k(owner_score, OWNERS // 2)[1].astype(jnp.int32)
    source = jnp.repeat(chosen, PAIR_CAP, axis=1)
    shuffle = jnp.argsort(jax.random.randint(subkeys[2], (OWNERS, KB), 0, KB) * KB + jnp.arange(KB, dtype=jnp.int32)[None, :], axis=1)
    source = jnp.take_along_axis(source, shuffle, axis=1).reshape(-1)
    onehot = (source[:, None] == jnp.arange(OWNERS, dtype=jnp.int32)[None, :]).astype(jnp.int32)
    earlier_count = jnp.sum((jnp.cumsum(onehot, axis=0) - onehot) * onehot, axis=1)
    slot_order = jnp.argsort(jax.random.randint(subkeys[3], (OWNERS, OB_DEV), 0, OB_DEV) * OB_DEV + jnp.arange(OB_DEV, dtype=jnp.int32)[None, :], axis=1)
    local_slot = slot_order[source, earlier_count]
    return (source * OB_DEV + local_slot).astype(jnp.int32)


def place_ends(result, stream_key, low, high):
    shape = result.shape
    place = [jax.random.randint(jax.random.fold_in(stream_key, axis), (), 0, shape[axis]) for axis in range(len(shape))]
    result = result.at[tuple(place)].set(low)
    longest = shape.index(max(shape))
    place[longest] = (place[longest] + 1) % shape[longest]
    return result.at[tuple(place)].set(high)


def block_scale(own_key, dims, pieces, smallest, largest):
    def one(position, shards_of):
        draws = jax.random.uniform(jax.random.fold_in(jax.random.fold_in(own_key, 6), position), (shards_of,), jnp.float32, smallest / len(pieces), largest / len(pieces))
        return jnp.repeat(jnp.exp(draws), dims[position] // shards_of).reshape((-1,) + (1,) * (len(dims) - position - 1))

    level = one(*pieces[0])
    for cut in pieces[1:]:
        level = level * one(*cut)
    return level


def normal_values(own_key, dims, width, bound, pieces=(), kind=jnp.bfloat16):
    entries = jax.random.normal(own_key, dims, jnp.float32) * width
    if len(pieces) > 0:
        entries = block_scale(own_key, dims, pieces, -0.22, 0.18) * entries
    return jnp.clip(entries, min=-bound, max=bound).astype(kind)


def setup_inputs(seed: int = 0, part: int = 0) -> dict:
    key_of = jax.random.split(jax.random.key(seed), 5)
    part_keys = jax.random.split(jax.random.fold_in(key_of[4], part), 5)
    return {
        "ocean_fields": draw_ocean_fields(jax.random.fold_in(jax.random.fold_in(key_of[4], part), 71), part),
        "stress_in": normal_values(part_keys[1], (3, NIR, NIC), 0.5, 3.0, ((1, 16),), jnp.float32),
        "ocean_slot": draw_ocean_slot(jax.random.fold_in(key_of[4], 71), part),
        "ice_mask": place_ends((jax.random.randint(key_of[3], (NI,), 0, 4) < 3).astype(jnp.int32), jax.random.fold_in(key_of[3], 1), 0, 1),
    }


EINV_SQ = 0.25
DELTA_MIN_SQ = 0.01
RELAXATION = 1.0
INV_STEP = 1.0
DRAG_COEFF = 0.5
CORIOLIS = 0.5
SPEED_MIN_SQ = 0.0025

def column_next(values):
    return jnp.roll(values, -1, axis=1)

def column_prev(values):
    return jnp.roll(values, 1, axis=1)

def padded_next(values):
    return jnp.concatenate([values[1:], jnp.zeros_like(values[:1])], axis=0)

def padded_prev(values):
    return jnp.concatenate([jnp.zeros_like(values[:1]), values[:-1]], axis=0)

def stress_section(vel_x, vel_y, stress_p, stress_m, stress_xy, strength, live_mask, row_next, row_prev):
    grad_ux = 0.5 * (column_next(vel_x) - column_prev(vel_x))
    grad_vy = 0.5 * (row_next(vel_y) - row_prev(vel_y))
    grad_uy = 0.5 * (row_next(vel_x) - row_prev(vel_x))
    grad_vx = 0.5 * (column_next(vel_y) - column_prev(vel_y))
    divergence = grad_ux + grad_vy
    tension = grad_ux - grad_vy
    shear_rate = grad_uy + grad_vx
    delta_rate = jnp.sqrt(divergence * divergence + (tension * tension + shear_rate * shear_rate) * EINV_SQ + DELTA_MIN_SQ)
    scaled = RELAXATION * strength / delta_rate
    new_p = live_mask * (stress_p + scaled * (divergence - delta_rate)) / (1.0 + RELAXATION)
    new_m = live_mask * (stress_m + scaled * tension * EINV_SQ) / (1.0 + RELAXATION)
    new_xy = live_mask * (stress_xy + scaled * shear_rate * (0.5 * EINV_SQ)) / (1.0 + RELAXATION)
    return (new_p, new_m, new_xy)

def momentum_section(vel_x, vel_y, stress_p, stress_m, stress_xy, ice_mass, wind_x, wind_y, current_x, current_y, cell_mask, row_valid, row_next, row_prev):
    normal_xx = 0.5 * (stress_p + stress_m)
    normal_yy = 0.5 * (stress_p - stress_m)
    force_x = 0.5 * (column_next(normal_xx) - column_prev(normal_xx)) + 0.5 * (row_next(stress_xy) - row_prev(stress_xy))
    force_y = 0.5 * (column_next(stress_xy) - column_prev(stress_xy)) + 0.5 * (row_next(normal_yy) - row_prev(normal_yy))
    rel_x = vel_x - current_x
    rel_y = vel_y - current_y
    drag_rate = DRAG_COEFF * jnp.sqrt(rel_x * rel_x + rel_y * rel_y + SPEED_MIN_SQ)
    inertia = ice_mass * INV_STEP
    diagonal = inertia + drag_rate
    turning = CORIOLIS * ice_mass
    rhs_x = inertia * vel_x + force_x + wind_x + drag_rate * current_x
    rhs_y = inertia * vel_y + force_y + wind_y + drag_rate * current_y
    determinant = diagonal * diagonal + turning * turning
    solved_x = (diagonal * rhs_x + turning * rhs_y) / determinant
    solved_y = (diagonal * rhs_y - turning * rhs_x) / determinant
    new_x = (cell_mask * solved_x + (1.0 - cell_mask) * current_x) * row_valid
    new_y = (cell_mask * solved_y + (1.0 - cell_mask) * current_y) * row_valid
    return (new_x, new_y)

def reference(ocean_fields, stress_in, ocean_slot, ice_mask):
    blocks = jnp.take(ocean_fields, ocean_slot.astype(jnp.int32), axis=1)
    ice_strip = blocks.reshape(8, OWNERS, KB, BY, BX).transpose(0, 1, 3, 2, 4).reshape(8, NIR, NIC)
    vel_x = ice_strip[0]
    vel_y = ice_strip[1]
    stress_p = stress_in[0]
    stress_m = stress_in[1]
    stress_xy = stress_in[2]
    mask_grid = ice_mask.reshape(OWNERS, KB).astype(jnp.float32)
    cell_mask = jnp.repeat(jnp.repeat(mask_grid, BY, axis=0), BX, axis=1)
    row_valid = 1.0
    for cycle_index in range(ITERS):
        stress_p, stress_m, stress_xy = stress_section(vel_x, vel_y, stress_p, stress_m, stress_xy, ice_strip[2], cell_mask * row_valid, padded_next, padded_prev)
        vel_x, vel_y = momentum_section(vel_x, vel_y, stress_p, stress_m, stress_xy, ice_strip[3], ice_strip[4], ice_strip[5], ice_strip[6], ice_strip[7], cell_mask, row_valid, padded_next, padded_prev)
    velocity = jnp.stack([vel_x, vel_y]).reshape(2, OWNERS, BY, KB, BX).transpose(0, 1, 3, 2, 4).reshape(2, NI, BY, BX)
    velocity_out = jnp.zeros((2, NOS, BY, BX), jnp.float32).at[:, ocean_slot.astype(jnp.int32)].set(velocity)
    return (velocity_out, jnp.stack([stress_p, stress_m, stress_xy]))
```

```python
import functools

import jax
import jax.numpy as jnp
from jax import lax
from jax.experimental import pallas as pl
from jax.experimental.pallas import tpu as pltpu
from jax.sharding import PartitionSpec as P

ITERS = 6
EINV_SQ = 0.25
DELTA_MIN_SQ = 0.01
DRAG_COEFF = 0.5
CORIOLIS = 0.5
SPEED_MIN_SQ = 0.0025


def index_tables(ocean_slot, owners, slot_count, per_owner, pair_cap, my_index):
    source = (ocean_slot // slot_count).reshape(owners, per_owner)
    place = (ocean_slot % slot_count).reshape(owners, per_owner)
    buffer_slots = owners * pair_cap
    earlier = jnp.arange(per_owner)[None, :] < jnp.arange(per_owner)[:, None]
    is_mine = source == my_index
    rank = jnp.sum(jnp.where(is_mine[:, None, :] & earlier[None], 1, 0), axis=2)
    hit = is_mine[:, :, None] & (rank[:, :, None] == jnp.arange(pair_cap)[None, None, :])
    send_index = (jnp.sum(jnp.where(hit, place[:, :, None] + 1, 0), axis=1) - 1).reshape(-1)
    slots = jnp.arange(slot_count)
    match = send_index[None, :] == slots[:, None]
    home_index = jnp.sum(jnp.where(match, jnp.arange(buffer_slots)[None, :] + 1, 0), axis=1) - 1
    mine = lax.dynamic_slice_in_dim(source, my_index, 1, 0)[0]
    my_rank = jnp.sum(jnp.where((mine[None, :] == mine[:, None]) & earlier, 1, 0), axis=1)
    receive_index = mine * pair_cap + my_rank
    back = receive_index[None, :] == jnp.arange(buffer_slots)[:, None]
    back_index = jnp.sum(jnp.where(back, jnp.arange(per_owner)[None, :], 0), axis=1)
    return jnp.concatenate(
        [jnp.maximum(send_index, 0), home_index, receive_index, back_index]
    ).astype(jnp.int32)


def kernel(
    owners, pair_cap, per_owner, slot_count,
    table, mask_ref, ocean, stress_in, vel_out, stress_out,
    send_buf, recv_buf, back_buf, home_buf, coef, vel, vel_blocks, mask_buf, edge, rim_send, rim_recv,
    send_sem, recv_sem, back_send_sem, back_recv_sem, rim_send_sem, rim_recv_sem,
):
    me = lax.axis_index("blk")
    cap = pair_cap
    positions = owners * cap
    home_at = positions
    receive_at = home_at + slot_count
    back_at = receive_at + per_owner
    cols = stress_in.shape[2]

    rim_recv[...] = jnp.zeros_like(rim_recv)
    barrier = pltpu.get_barrier_semaphore()

    def greet(k, _):
        pl.semaphore_signal(
            barrier, inc=1, device_id={"blk": lax.rem(me + k, owners)},
            device_id_type=pl.DeviceIdType.MESH,
        )
        return 0

    lax.fori_loop(1, owners, greet, 0)
    pl.semaphore_wait(barrier, owners - 1)

    def out_copy(peer):
        return pltpu.make_async_remote_copy(
            src_ref=send_buf.at[pl.ds(peer * cap, cap)],
            dst_ref=recv_buf.at[pl.ds(me * cap, cap)],
            send_sem=send_sem.at[peer],
            recv_sem=recv_sem.at[me],
            device_id={"blk": peer},
            device_id_type=pl.DeviceIdType.MESH,
        )

    def in_copy(peer):
        return pltpu.make_async_remote_copy(
            src_ref=send_buf.at[pl.ds(me * cap, cap)],
            dst_ref=recv_buf.at[pl.ds(peer * cap, cap)],
            send_sem=send_sem.at[me],
            recv_sem=recv_sem.at[peer],
            device_id={"blk": peer},
            device_id_type=pl.DeviceIdType.MESH,
        )

    def send_to(k, _):
        peer = lax.rem(me + k, owners)
        for r in range(cap):
            at = peer * cap + r
            send_buf[at] = ocean[:, table[at]]
        out_copy(peer).start()
        return 0

    half = owners // 2
    lax.fori_loop(half, owners, send_to, 0)
    lax.fori_loop(1, half, send_to, 0)
    for r in range(cap):
        at = me * cap + r
        recv_buf[at] = ocean[:, table[at]]

    row = lax.broadcasted_iota(jnp.int32, (8, 128), 0)
    above = lax.max(me - 1, 0)
    below = lax.min(me + 1, owners - 1)
    above_ok = jnp.where(me > 0, 1.0, 0.0)
    below_ok = jnp.where(me < owners - 1, 1.0, 0.0)

    def mask_block(j, _):
        at = pl.ds(pl.multiple_of(j * 128, 128), 128)
        mask_buf[0, :, at] = jnp.full((8, 128), mask_ref[me * per_owner + j].astype(jnp.float32))
        low = mask_ref[below * per_owner + j].astype(jnp.float32) * below_ok
        high = mask_ref[above * per_owner + j].astype(jnp.float32) * above_ok
        mask_buf[1, :, at] = jnp.where(row < 4, low, high)
        return 0

    lax.fori_loop(0, per_owner, mask_block, 0)
    stress_out[...] = stress_in[...]

    def arrived(k, _):
        in_copy(lax.rem(me + k, owners)).wait_recv()
        return 0

    lax.fori_loop(1, owners, arrived, 0)

    def unpack(j, _):
        at = pl.ds(pl.multiple_of(j * 128, 128), 128)
        block = recv_buf[table[receive_at + j]]
        vel[0, :, at] = block[0]
        vel[1, :, at] = block[1]
        for f in range(6):
            coef[f, :, at] = block[2 + f]
        return 0

    lax.fori_loop(0, per_owner, unpack, 0)

    rows = lax.broadcasted_iota(jnp.int32, (8, cols), 0)

    def rim_copies(slot, up):
        side = 0 if up else 1
        peer = lax.max(me - 1, 0) if up else lax.min(me + 1, owners - 1)
        return pltpu.make_async_remote_copy(
            src_ref=rim_send.at[slot, side],
            dst_ref=rim_recv.at[slot, side],
            send_sem=rim_send_sem.at[slot, side],
            recv_sem=rim_recv_sem.at[slot, side],
            device_id={"blk": peer},
            device_id_type=pl.DeviceIdType.MESH,
        )

    def rim_start(slot):
        @pl.when(me > 0)
        def _():
            rim_copies(slot, True).start()

        @pl.when(me < owners - 1)
        def _():
            rim_copies(slot, False).start()

    def rim_wait(slot):
        @pl.when(me < owners - 1)
        def _():
            rim_copies(slot, True).wait_recv()

        @pl.when(me > 0)
        def _():
            rim_copies(slot, False).wait_recv()

    def rim_drain(slot):
        @pl.when(me > 0)
        def _():
            rim_copies(slot, True).wait_send()

        @pl.when(me < owners - 1)
        def _():
            rim_copies(slot, False).wait_send()

    def rim_tile(slot):
        return jnp.concatenate([rim_recv[slot, 0], rim_recv[slot, 1]], axis=0)

    def send_velocity(slot):
        rim_send[slot, 0, 0:2] = vel[0, 0:2]
        rim_send[slot, 0, 2:4] = vel[1, 0:2]
        rim_send[slot, 1, 0:2] = vel[1, 6:8]
        rim_send[slot, 1, 2:4] = vel[0, 6:8]
        rim_start(slot)

    def pick(tile, shift):
        return jnp.where(rows < 4, pltpu.roll(tile, 8 - shift, 0), pltpu.roll(tile, shift, 0))

    for f, (low, high) in enumerate(
        ((coef.at[0], coef.at[0]), *((stress_out.at[s], stress_out.at[s]) for s in range(3)))
    ):
        rim_send[ITERS, 0, f : f + 1] = low[0:1]
        rim_send[ITERS, 1, 3 - f : 4 - f] = high[7:8]
    rim_start(ITERS)
    send_velocity(0)
    rim_wait(ITERS)
    first = rim_tile(ITERS)
    edge[0] = first
    for s in range(3):
        edge[s + 1] = pick(first, s + 1)

    def east(a):
        return pltpu.roll(a, cols - 1, 1)

    def west(a):
        return pltpu.roll(a, 1, 1)

    def both_next(a, h):
        ra, rh = pltpu.roll(a, 7, 0), pltpu.roll(h, 7, 0)
        return jnp.where(rows == 7, rh, ra), jnp.where(rows == 7, ra, rh)

    def both_prev(a, h):
        ra, rh = pltpu.roll(a, 1, 0), pltpu.roll(h, 1, 0)
        return jnp.where(rows == 0, rh, ra), jnp.where(rows == 0, ra, rh)

    def stresses(vx, vy, nx, sx, ny, sy, p, m, xy, strength, mask):
        gux = 0.5 * (east(vx) - west(vx))
        gvx = 0.5 * (east(vy) - west(vy))
        gvy = 0.5 * (ny - sy)
        guy = 0.5 * (nx - sx)
        divergence = gux + gvy
        tension = gux - gvy
        shear = guy + gvx
        q = (
            divergence * divergence
            + (tension * tension + shear * shear) * EINV_SQ
            + DELTA_MIN_SQ
        )
        inv = lax.rsqrt(q)
        scaled = strength * inv
        half_mask = 0.5 * mask
        new_p = half_mask * (p + scaled * (divergence - q * inv))
        new_m = half_mask * (m + scaled * tension * EINV_SQ)
        new_xy = half_mask * (xy + scaled * shear * (0.5 * EINV_SQ))
        return new_p, new_m, new_xy

    def subcycle(t, _):
        rim_wait(t)
        vx, vy = vel[0], vel[1]
        hx = rim_tile(t)
        hy = pick(hx, 2)
        nx, hnx = both_next(vx, hx)
        sx, hsx = both_prev(vx, hx)
        ny, hny = both_next(vy, hy)
        sy, hsy = both_prev(vy, hy)
        mask = mask_buf[0]
        p, m, xy = stresses(
            vx, vy, nx, sx, ny, sy, stress_out[0], stress_out[1], stress_out[2], coef[0], mask
        )
        hp, hm, hxy = stresses(
            hx, hy, hnx, hsx, hny, hsy, edge[1], edge[2], edge[3], edge[0], mask_buf[1]
        )
        stress_out[0] = p
        stress_out[1] = m
        stress_out[2] = xy
        edge[1] = hp
        edge[2] = hm
        edge[3] = hxy
        sxx = 0.5 * (p + m)
        syy = 0.5 * (p - m)
        hyy = 0.5 * (hp - hm)
        force_x = 0.5 * (east(sxx) - west(sxx)) + 0.5 * (
            both_next(xy, hxy)[0] - both_prev(xy, hxy)[0]
        )
        force_y = 0.5 * (east(xy) - west(xy)) + 0.5 * (
            both_next(syy, hyy)[0] - both_prev(syy, hyy)[0]
        )
        mass, wx, wy, cx, cy = coef[1], coef[2], coef[3], coef[4], coef[5]
        rel_x = vx - cx
        rel_y = vy - cy
        q = rel_x * rel_x + rel_y * rel_y + SPEED_MIN_SQ
        drag = DRAG_COEFF * (q * lax.rsqrt(q))
        diag = mass + drag
        turning = CORIOLIS * mass
        rhs_x = mass * vx + force_x + wx + drag * cx
        rhs_y = mass * vy + force_y + wy + drag * cy
        inv_det = 1.0 / (diag * diag + turning * turning)
        vel[0] = mask * ((diag * rhs_x + turning * rhs_y) * inv_det) + (1.0 - mask) * cx
        vel[1] = mask * ((diag * rhs_y - turning * rhs_x) * inv_det) + (1.0 - mask) * cy

        @pl.when(t < ITERS - 1)
        def _():
            send_velocity(t + 1)

        return 0

    lax.fori_loop(0, ITERS, subcycle, 0)

    def to_blocks(j, _):
        at = pl.ds(pl.multiple_of(j * 128, 128), 128)
        vel_blocks[j, 0] = vel[0, :, at]
        vel_blocks[j, 1] = vel[1, :, at]
        return 0

    lax.fori_loop(0, per_owner, to_blocks, 0)

    def back_copy(peer):
        return pltpu.make_async_remote_copy(
            src_ref=back_buf.at[pl.ds(peer * cap, cap)],
            dst_ref=home_buf.at[pl.ds(me * cap, cap)],
            send_sem=back_send_sem.at[peer],
            recv_sem=back_recv_sem.at[me],
            device_id={"blk": peer},
            device_id_type=pl.DeviceIdType.MESH,
        )

    def home_copy(peer):
        return pltpu.make_async_remote_copy(
            src_ref=back_buf.at[pl.ds(me * cap, cap)],
            dst_ref=home_buf.at[pl.ds(peer * cap, cap)],
            send_sem=back_send_sem.at[me],
            recv_sem=back_recv_sem.at[peer],
            device_id={"blk": peer},
            device_id_type=pl.DeviceIdType.MESH,
        )

    def send_back(k, _):
        peer = lax.rem(me + k, owners)
        for r in range(cap):
            at = peer * cap + r
            back_buf[at] = vel_blocks[table[back_at + at]]
        back_copy(peer).start()
        return 0

    lax.fori_loop(half, owners, send_back, 0)
    lax.fori_loop(1, half, send_back, 0)
    for r in range(cap):
        at = me * cap + r
        home_buf[at] = vel_blocks[table[back_at + at]]

    def drain(k, _):
        out_copy(lax.rem(me + k, owners)).wait_send()
        return 0

    lax.fori_loop(1, owners, drain, 0)
    lax.fori_loop(0, ITERS + 1, lambda t, _: (rim_drain(t), 0)[1], 0)

    def came_home(k, _):
        home_copy(lax.rem(me + k, owners)).wait_recv()
        return 0

    lax.fori_loop(1, owners, came_home, 0)

    def place(slot, _):
        at = table[home_at + slot]
        block = home_buf[lax.max(at, 0)]
        held = jnp.full((8, 128), at, jnp.int32) >= 0
        vel_out[0, slot] = jnp.where(held, block[0], 0.0)
        vel_out[1, slot] = jnp.where(held, block[1], 0.0)
        return 0

    lax.fori_loop(0, slot_count, place, 0)

    def back_drain(k, _):
        back_copy(lax.rem(me + k, owners)).wait_send()
        return 0

    lax.fori_loop(1, owners, back_drain, 0)


def per_device(ocean_fields, stress_in, ocean_slot, ice_mask):
    owners = lax.axis_size("blk")
    my_index = lax.axis_index("blk")
    field_count, slot_count, block_rows, block_cols = ocean_fields.shape
    strip_cols = stress_in.shape[2]
    per_owner = strip_cols // block_cols
    pair_cap = 2 * per_owner // owners
    positions = owners * pair_cap
    table = index_tables(ocean_slot, owners, slot_count, per_owner, pair_cap, my_index)
    block = (block_rows, block_cols)
    strip = (block_rows, strip_cols)
    f32 = jnp.float32
    vmem = pl.BlockSpec(memory_space=pltpu.VMEM)
    smem = pl.BlockSpec(memory_space=pltpu.SMEM)
    return pl.pallas_call(
        functools.partial(kernel, owners, pair_cap, per_owner, slot_count),
        out_shape=(
            jax.ShapeDtypeStruct((2, slot_count) + block, f32),
            jax.ShapeDtypeStruct((3,) + strip, f32),
        ),
        in_specs=[smem, smem, vmem, vmem],
        out_specs=(vmem, vmem),
        scratch_shapes=[
            pltpu.VMEM((positions, field_count) + block, f32),
            pltpu.VMEM((positions, field_count) + block, f32),
            pltpu.VMEM((positions, 2) + block, f32),
            pltpu.VMEM((positions, 2) + block, f32),
            pltpu.VMEM((6,) + strip, f32),
            pltpu.VMEM((2,) + strip, f32),
            pltpu.VMEM((per_owner, 2) + block, f32),
            pltpu.VMEM((2,) + strip, f32),
            pltpu.VMEM((4,) + strip, f32),
            pltpu.VMEM((ITERS + 1, 2, 4, strip_cols), f32),
            pltpu.VMEM((ITERS + 1, 2, 4, strip_cols), f32),
            pltpu.SemaphoreType.DMA((owners,)),
            pltpu.SemaphoreType.DMA((owners,)),
            pltpu.SemaphoreType.DMA((owners,)),
            pltpu.SemaphoreType.DMA((owners,)),
            pltpu.SemaphoreType.DMA((ITERS + 1, 2)),
            pltpu.SemaphoreType.DMA((ITERS + 1, 2)),
        ],
        compiler_params=pltpu.CompilerParams(
            collective_id=0, has_side_effects=True, vmem_limit_bytes=40 * 1024 * 1024
        ),
    )(table, ice_mask, ocean_fields, stress_in)


def solution(mesh):
    placed = (P(None, ("groups", "blk"), None, None), P(None, ("groups", "blk"), None), P(), P())
    return jax.shard_map(
        per_device,
        mesh=mesh,
        in_specs=placed,
        out_specs=(P(None, ("groups", "blk"), None, None), P(None, ("groups", "blk"), None)),
        check_vma=False,
    )
```

```python
import functools

import jax
import jax.numpy as jnp
from jax import lax
from jax.experimental import pallas as pl
from jax.experimental.pallas import tpu as pltpu
from jax.sharding import PartitionSpec as P

ITERS = 6
EINV_SQ = 0.25
DELTA_MIN_SQ = 0.01
DRAG_COEFF = 0.5
CORIOLIS = 0.5
SPEED_MIN_SQ = 0.0025


def index_tables(ocean_slot, owners, slot_count, per_owner, pair_cap, my_index):
    source = (ocean_slot // slot_count).reshape(owners, per_owner)
    place = (ocean_slot % slot_count).reshape(owners, per_owner)
    buffer_slots = owners * pair_cap
    earlier = jnp.arange(per_owner)[None, :] < jnp.arange(per_owner)[:, None]
    is_mine = source == my_index
    rank = jnp.sum(jnp.where(is_mine[:, None, :] & earlier[None], 1, 0), axis=2)
    hit = is_mine[:, :, None] & (rank[:, :, None] == jnp.arange(pair_cap)[None, None, :])
    send_index = (jnp.sum(jnp.where(hit, place[:, :, None] + 1, 0), axis=1) - 1).reshape(-1)
    slots = jnp.arange(slot_count)
    match = send_index[None, :] == slots[:, None]
    home_index = jnp.sum(jnp.where(match, jnp.arange(buffer_slots)[None, :] + 1, 0), axis=1) - 1
    mine = lax.dynamic_slice_in_dim(source, my_index, 1, 0)[0]
    my_rank = jnp.sum(jnp.where((mine[None, :] == mine[:, None]) & earlier, 1, 0), axis=1)
    receive_index = mine * pair_cap + my_rank
    back = receive_index[None, :] == jnp.arange(buffer_slots)[:, None]
    back_index = jnp.sum(jnp.where(back, jnp.arange(per_owner)[None, :], 0), axis=1)
    return jnp.concatenate(
        [jnp.maximum(send_index, 0), home_index, receive_index, back_index]
    ).astype(jnp.int32)


def kernel(
    owners, pair_cap, per_owner, slot_count,
    table, mask_ref, ocean_hbm, stress_in, vel_out, stress_out,
    ocean, send_a, send_b, recv_a, recv_b, back_buf, home_buf, coef, vel, vel_blocks, mask_buf, edge, solve,
    rim_send, rim_recv,
    load_sem, send_sem, recv_sem, back_send_sem, back_recv_sem, rim_send_sem, rim_recv_sem,
):
    me = lax.axis_index("blk")
    cap = pair_cap
    home_at = owners * cap
    receive_at = home_at + slot_count
    back_at = receive_at + per_owner
    cols = stress_in.shape[2]
    first_count = send_a.shape[1]

    load_ocean = pltpu.make_async_copy(ocean_hbm, ocean, load_sem.at[0])
    load_stress = pltpu.make_async_copy(stress_in, stress_out, load_sem.at[1])
    load_ocean.start()
    load_stress.start()
    rim_recv[...] = jnp.zeros_like(rim_recv)
    barrier = pltpu.get_barrier_semaphore()

    def greet(k, _):
        pl.semaphore_signal(
            barrier, inc=1, device_id={"blk": lax.rem(me + k, owners)},
            device_id_type=pl.DeviceIdType.MESH,
        )
        return 0

    lax.fori_loop(1, owners, greet, 0)

    row = lax.broadcasted_iota(jnp.int32, (8, 128), 0)
    above = lax.max(me - 1, 0)
    below = lax.min(me + 1, owners - 1)
    above_ok = jnp.where(me > 0, 1.0, 0.0)
    below_ok = jnp.where(me < owners - 1, 1.0, 0.0)

    def mask_block(j, _):
        at = pl.ds(pl.multiple_of(j * 128, 128), 128)
        own = mask_ref[me * per_owner + j].astype(jnp.float32)
        mask_buf[0, :, at] = jnp.full((8, 128), own)
        low = mask_ref[below * per_owner + j].astype(jnp.float32) * below_ok
        high = mask_ref[above * per_owner + j].astype(jnp.float32) * above_ok
        mask_buf[1, :, at] = jnp.where(row < 2, high, jnp.where(row < 6, own, low))
        return 0

    lax.fori_loop(0, per_owner, mask_block, 0)
    load_ocean.wait()
    pl.semaphore_wait(barrier, owners - 1)

    def pair_copy(part, source, dest):
        src, dst = (send_a, recv_a) if part == 0 else (send_b, recv_b)
        return pltpu.make_async_remote_copy(
            src_ref=src.at[pl.ds(dest * cap, cap)],
            dst_ref=dst.at[pl.ds(source * cap, cap)],
            send_sem=send_sem.at[part, dest],
            recv_sem=recv_sem.at[part, source],
            device_id={"blk": lax.rem(dest + source - me + owners, owners)},
            device_id_type=pl.DeviceIdType.MESH,
        )

    def send_first(k, _):
        peer = lax.rem(me + k, owners)
        for r in range(cap):
            at = peer * cap + r
            send_a[at] = ocean[0:first_count, table[at]]
        pair_copy(0, me, peer).start()
        return 0

    def send_second(k, _):
        peer = lax.rem(me + k, owners)
        for r in range(cap):
            at = peer * cap + r
            send_b[at] = ocean[first_count:, table[at]]
        pair_copy(1, me, peer).start()
        return 0

    half = owners // 2
    for send in (send_first, send_second):
        lax.fori_loop(half, owners, send, 0)
        lax.fori_loop(1, half, send, 0)
    for r in range(cap):
        at = me * cap + r
        recv_a[at] = ocean[0:first_count, table[at]]
        recv_b[at] = ocean[first_count:, table[at]]
    load_stress.wait()

    def wait_first(k, _):
        pair_copy(0, lax.rem(me + k, owners), me).wait_recv()
        return 0

    def wait_second(k, _):
        pair_copy(1, lax.rem(me + k, owners), me).wait_recv()
        return 0

    def unpack_first(j, _):
        at = pl.ds(pl.multiple_of(j * 128, 128), 128)
        block = recv_a[table[receive_at + j]]
        vel[0, :, at] = block[0]
        vel[1, :, at] = block[1]
        coef[0, :, at] = block[2]
        return 0

    def unpack_second(j, _):
        at = pl.ds(pl.multiple_of(j * 128, 128), 128)
        block = recv_b[table[receive_at + j]]
        for f in range(5):
            coef[1 + f, :, at] = block[f]
        return 0

    lax.fori_loop(1, owners, wait_first, 0)
    lax.fori_loop(0, per_owner, unpack_first, 0)

    rows = lax.broadcasted_iota(jnp.int32, (8, cols), 0)

    def rim_copy(slot, side):
        peer = above if side == 0 else below
        return pltpu.make_async_remote_copy(
            src_ref=rim_send.at[slot, side],
            dst_ref=rim_recv.at[slot, side],
            send_sem=rim_send_sem.at[slot, side],
            recv_sem=rim_recv_sem.at[slot, side],
            device_id={"blk": peer},
            device_id_type=pl.DeviceIdType.MESH,
        )

    def rim_start(slot):
        @pl.when(me > 0)
        def _():
            rim_copy(slot, 0).start()

        @pl.when(me < owners - 1)
        def _():
            rim_copy(slot, 1).start()

    def rim_wait(slot):
        @pl.when(me < owners - 1)
        def _():
            rim_copy(slot, 0).wait_recv()

        @pl.when(me > 0)
        def _():
            rim_copy(slot, 1).wait_recv()

    def rim_drain(slot):
        @pl.when(me > 0)
        def _():
            rim_copy(slot, 0).wait_send()

        @pl.when(me < owners - 1)
        def _():
            rim_copy(slot, 1).wait_send()

    def rim_tile(slot):
        return jnp.concatenate([rim_recv[slot, 1], rim_recv[slot, 0]], axis=0)

    def send_velocity(slot):
        rim_send[slot, 0, 0:2] = vel[1, 0:2]
        rim_send[slot, 0, 2:4] = vel[0, 0:2]
        rim_send[slot, 1, 0:2] = vel[0, 6:8]
        rim_send[slot, 1, 2:4] = vel[1, 6:8]
        rim_start(slot)

    def turn(tile, shift):
        return pltpu.roll(tile, shift % 8, 0) if shift % 8 else tile

    def halves(tile, upper, lower):
        return jnp.where(rows < 4, turn(tile, upper), turn(tile, lower))

    def packed(own, rim):
        return jnp.where((rows >= 2) & (rows < 6), halves(own, 2, -2), rim)

    for f, field in enumerate((coef.at[0], *(stress_out.at[s] for s in range(3)))):
        rim_send[ITERS, 0, 3 - f : 4 - f] = field[0:1]
        rim_send[ITERS, 1, f : f + 1] = field[7:8]
    rim_start(ITERS)
    send_velocity(0)
    rim_wait(ITERS)
    first = rim_tile(ITERS)
    for f, field in enumerate((coef.at[0], *(stress_out.at[s] for s in range(3)))):
        edge[f] = packed(field[...], halves(first, 1 - f, f - 1))

    def east(a):
        return pltpu.roll(a, cols - 1, 1)

    def west(a):
        return pltpu.roll(a, 1, 1)

    def stresses(vx, vy, p, m, xy, strength, mask):
        gux = 0.5 * (east(vx) - west(vx))
        gvx = 0.5 * (east(vy) - west(vy))
        gvy = 0.5 * (turn(vy, -1) - turn(vy, 1))
        guy = 0.5 * (turn(vx, -1) - turn(vx, 1))
        divergence = gux + gvy
        tension = gux - gvy
        shear = guy + gvx
        q = (
            divergence * divergence
            + (tension * tension + shear * shear) * EINV_SQ
            + DELTA_MIN_SQ
        )
        inv = lax.rsqrt(q)
        scaled = strength * inv
        half_mask = 0.5 * mask
        new_p = half_mask * (p + scaled * (divergence - q * inv))
        new_m = half_mask * (m + scaled * tension * EINV_SQ)
        new_xy = half_mask * (xy + scaled * shear * (0.5 * EINV_SQ))
        return new_p, new_m, new_xy

    def prepare():
        vx, vy, mask = vel[0], vel[1], mask_buf[0]
        mass, wx, wy, cx, cy = coef[1], coef[2], coef[3], coef[4], coef[5]
        rel_x = vx - cx
        rel_y = vy - cy
        q = rel_x * rel_x + rel_y * rel_y + SPEED_MIN_SQ
        drag = DRAG_COEFF * (q * lax.rsqrt(q))
        diag = mass + drag
        turning = CORIOLIS * mass
        base_x = mass * vx + wx + drag * cx
        base_y = mass * vy + wy + drag * cy
        inv_det = mask / (diag * diag + turning * turning)
        along = diag * inv_det
        across = turning * inv_det
        solve[0] = along
        solve[1] = across
        solve[2] = along * base_x + across * base_y + (1.0 - mask) * cx
        solve[3] = along * base_y - across * base_x + (1.0 - mask) * cy

    def subcycle(t, _):
        inner = stresses(
            vel[0], vel[1], stress_out[0], stress_out[1], stress_out[2], coef[0], mask_buf[0]
        )
        for s in range(3):
            stress_out[s] = inner[s]

        @pl.when(t > 0)
        def _():
            prepare()

        rim_wait(t)
        rim = rim_tile(t)
        outer = stresses(
            packed(vel[0], rim),
            packed(vel[1], halves(rim, -2, 2)),
            edge[1], edge[2], edge[3], edge[0], mask_buf[1],
        )
        for s in range(3):
            edge[s + 1] = outer[s]
            stress_out[s] = jnp.where(
                rows == 0, turn(outer[s], -2), jnp.where(rows == 7, turn(outer[s], 2), stress_out[s])
            )

        @pl.when(t == 0)
        def _():
            lax.fori_loop(1, owners, wait_second, 0)
            lax.fori_loop(0, per_owner, unpack_second, 0)
            prepare()

        def across_rows(own, beside):
            above_it = jnp.where(rows == 7, turn(beside, 1), turn(own, -1))
            below_it = jnp.where(rows == 0, turn(beside, -1), turn(own, 1))
            return above_it - below_it

        p, m, xy = stress_out[0], stress_out[1], stress_out[2]
        sxx = 0.5 * (p + m)
        syy = 0.5 * (p - m)
        beside_yy = 0.5 * (edge[1] - edge[2])
        force_x = 0.5 * (east(sxx) - west(sxx)) + 0.5 * across_rows(xy, edge[3])
        force_y = 0.5 * (east(xy) - west(xy)) + 0.5 * across_rows(syy, beside_yy)
        vel[0] = solve[0] * force_x + solve[1] * force_y + solve[2]
        vel[1] = solve[0] * force_y - solve[1] * force_x + solve[3]

        @pl.when(t < ITERS - 1)
        def _():
            send_velocity(t + 1)

        return 0

    lax.fori_loop(0, ITERS, subcycle, 0)

    def to_blocks(j, _):
        at = pl.ds(pl.multiple_of(j * 128, 128), 128)
        vel_blocks[j, 0] = vel[0, :, at]
        vel_blocks[j, 1] = vel[1, :, at]
        return 0

    lax.fori_loop(0, per_owner, to_blocks, 0)

    def back_copy(source, dest):
        return pltpu.make_async_remote_copy(
            src_ref=back_buf.at[pl.ds(dest * cap, cap)],
            dst_ref=home_buf.at[pl.ds(source * cap, cap)],
            send_sem=back_send_sem.at[dest],
            recv_sem=back_recv_sem.at[source],
            device_id={"blk": lax.rem(dest + source - me + owners, owners)},
            device_id_type=pl.DeviceIdType.MESH,
        )

    def send_back(k, _):
        peer = lax.rem(me + k, owners)
        for r in range(cap):
            at = peer * cap + r
            back_buf[at] = vel_blocks[table[back_at + at]]
        back_copy(me, peer).start()
        return 0

    lax.fori_loop(half, owners, send_back, 0)
    lax.fori_loop(1, half, send_back, 0)
    for r in range(cap):
        at = me * cap + r
        home_buf[at] = vel_blocks[table[back_at + at]]

    def drain(k, _):
        pair_copy(0, me, lax.rem(me + k, owners)).wait_send()
        pair_copy(1, me, lax.rem(me + k, owners)).wait_send()
        return 0

    lax.fori_loop(1, owners, drain, 0)
    lax.fori_loop(0, ITERS + 1, lambda t, _: (rim_drain(t), 0)[1], 0)

    def came_home(k, _):
        back_copy(lax.rem(me + k, owners), me).wait_recv()
        return 0

    lax.fori_loop(1, owners, came_home, 0)

    def place(slot, _):
        at = table[home_at + slot]
        block = home_buf[lax.max(at, 0)]
        held = jnp.full((8, 128), at, jnp.int32) >= 0
        vel_out[0, slot] = jnp.where(held, block[0], 0.0)
        vel_out[1, slot] = jnp.where(held, block[1], 0.0)
        return 0

    lax.fori_loop(0, slot_count, place, 0)

    def back_drain(k, _):
        back_copy(me, lax.rem(me + k, owners)).wait_send()
        return 0

    lax.fori_loop(1, owners, back_drain, 0)


def per_device(ocean_fields, stress_in, ocean_slot, ice_mask):
    owners = lax.axis_size("blk")
    my_index = lax.axis_index("blk")
    field_count, slot_count, block_rows, block_cols = ocean_fields.shape
    strip_cols = stress_in.shape[2]
    per_owner = strip_cols // block_cols
    pair_cap = 2 * per_owner // owners
    positions = owners * pair_cap
    table = index_tables(ocean_slot, owners, slot_count, per_owner, pair_cap, my_index)
    block = (block_rows, block_cols)
    strip = (block_rows, strip_cols)
    f32 = jnp.float32
    vmem = pl.BlockSpec(memory_space=pltpu.VMEM)
    smem = pl.BlockSpec(memory_space=pltpu.SMEM)
    anywhere = pl.BlockSpec(memory_space=pl.ANY)
    first_count = 3
    rest_count = field_count - first_count
    return pl.pallas_call(
        functools.partial(kernel, owners, pair_cap, per_owner, slot_count),
        out_shape=(
            jax.ShapeDtypeStruct((2, slot_count) + block, f32),
            jax.ShapeDtypeStruct((3,) + strip, f32),
        ),
        in_specs=[smem, smem, anywhere, anywhere],
        out_specs=(vmem, vmem),
        scratch_shapes=[
            pltpu.VMEM((field_count, slot_count) + block, f32),
            pltpu.VMEM((positions, first_count) + block, f32),
            pltpu.VMEM((positions, rest_count) + block, f32),
            pltpu.VMEM((positions, first_count) + block, f32),
            pltpu.VMEM((positions, rest_count) + block, f32),
            pltpu.VMEM((positions, 2) + block, f32),
            pltpu.VMEM((positions, 2) + block, f32),
            pltpu.VMEM((6,) + strip, f32),
            pltpu.VMEM((2,) + strip, f32),
            pltpu.VMEM((per_owner, 2) + block, f32),
            pltpu.VMEM((2,) + strip, f32),
            pltpu.VMEM((4,) + strip, f32),
            pltpu.VMEM((4,) + strip, f32),
            pltpu.VMEM((ITERS + 1, 2, 4, strip_cols), f32),
            pltpu.VMEM((ITERS + 1, 2, 4, strip_cols), f32),
            pltpu.SemaphoreType.DMA((2,)),
            pltpu.SemaphoreType.DMA((2, owners)),
            pltpu.SemaphoreType.DMA((2, owners)),
            pltpu.SemaphoreType.DMA((owners,)),
            pltpu.SemaphoreType.DMA((owners,)),
            pltpu.SemaphoreType.DMA((ITERS + 1, 2)),
            pltpu.SemaphoreType.DMA((ITERS + 1, 2)),
        ],
        compiler_params=pltpu.CompilerParams(
            collective_id=0, has_side_effects=True, vmem_limit_bytes=40 * 1024 * 1024
        ),
    )(table, ice_mask, ocean_fields, stress_in)


def solution(mesh):
    placed = (P(None, ("groups", "blk"), None, None), P(None, ("groups", "blk"), None), P(), P())
    return jax.shard_map(
        per_device,
        mesh=mesh,
        in_specs=placed,
        out_specs=(P(None, ("groups", "blk"), None, None), P(None, ("groups", "blk"), None)),
        check_vma=False,
    )
```
